128 devices in a mesh: gx: 16 (over x, y), gy: 8 (over z, core).
Axes of the slice: x: 4, y: 4, z: 4, core: 2. Of those that a mesh axis runs over, the one named last changes fastest.
Arguments:
- state: bfloat16 [64, 24, 192, 256], P('gx', 'gy'), may hold values from -1 to 1
- weights: bfloat16 [64, 24, 9, 256, 256], P('gx', 'gy'), may hold values from -0.125 to 0.125
- drive: bfloat16 [2, 64, 24, 192, 256], P(None, 'gx', 'gy'), may hold values from -6 to 6
- leak: float32 [64, 24, 256], P('gx', 'gy'), may hold values from 0.1 to 1
- link_dev: int32 [16, 8, 12, 3], P(None, 'gy'), may hold values from 0 to 15, all different within a row; in each aligned block of 12 rows (0 to 11, 12 to 23, ..., all dimensions but the last counted through in order) at most 4 rows name the same one
- link_blk: int32 [16, 8, 12, 3], P(None, 'gy'), may hold values from 0 to 11
- offsets: int32 [5, 2], replicated, may hold values from -1 to 1, as said below
- gram_prev: float32 [64, 24, 256, 256], P('gx', 'gy'), may hold values from -6 to 6
Outputs:
- final_state: bfloat16 [64, 24, 192, 256], P('gx', 'gy')
- gram: float32 [64, 24, 256, 256], P('gx', 'gy')
The draws below stay inside these ranges and needn't reach their ends.
Inputs may be any that keep to these rules, and one draw needn't show every extreme that they name: `link_dev`: the 3 sources of one block lie on different indices of gx; among the blocks of one device at most 4 sources lie on any one index of gx, and exactly 4 on some. Five distinct offsets.
All inputs are finite; a program needn't handle non-finite values.
Results may differ from the reference program's by a relative error of at most 0.0046.
Values may be sent and summed in bfloat16 or wider, within the bound.
No kernel may reach another device: no remote copies, remote signals or barrier semaphores. Data moves between devices by JAX's collectives and lax.ppermute only.
A program may use at most 192 MiB of HBM per device.

```python
import math
import jax
import jax.numpy as jnp
import numpy as np
from jax import lax

U = 256
LINKS = 3
STENCIL = 5
STEPS = 2
R = 4
C = 3
SEQ = 192
CAP = 4
NBR = 64
NBC = 24
N_GX = 16
N_GY = 8


def draw_offsets(key, part):
    chosen = jax.random.permutation(key, 9)[:STENCIL]
    return jnp.stack([chosen // 3 - 1, chosen % 3 - 1], axis=1).astype(jnp.int32)


def place_ends(drawn, stream_key, smallest, top_value):
    extent = drawn.shape
    place = [jax.random.randint(jax.random.fold_in(stream_key, axis), (), 0, extent[axis]) for axis in range(len(extent))]
    drawn = drawn.at[tuple(place)].set(smallest)
    longest = extent.index(max(extent))
    place[longest] = (place[longest] + 1) % extent[longest]
    return drawn.at[tuple(place)].set(top_value)


def levels(rng, extent, split, smallest, high):
    loudness, own = 1.0, jax.random.fold_in(rng, 6)
    for position, shards_of in split:
        steps = jnp.exp(jax.random.uniform(jax.random.fold_in(own, position), (shards_of,), jnp.float32, smallest / len(split), high / len(split)))
        loudness = loudness * jnp.repeat(steps, extent[position] // shards_of).reshape([-1 if axis == position else 1 for axis in range(len(extent))])
    return loudness


def routed_block(key, own, number, rows, number_of, top, most, slope):
    sequence = jax.random.permutation(key, number_of)
    packed, common = portions_of(number_of, rows * top, most, slope, True), portions_of(number_of, rows * top, most, slope, False)
    places = jnp.arange(number_of)

    def named(sizes, turn):
        used = int((sizes > 0).sum())
        fixed = max(1, used // 4)
        passed = fixed + (places - fixed + turn * (used - fixed)) % max(1, number_of - fixed)
        return jnp.zeros((number_of,), jnp.int32).at[sequence[jnp.where(places < fixed, places, passed)]].set(jnp.asarray(sizes, jnp.int32))

    sizes = jnp.where(number % 4 == 0, named(packed, number // 4), named(common, number - number // 4 - 1))
    mixed = jax.random.permutation(jax.random.fold_in(own, 3), number_of)
    giver, taker = mixed[0:number_of // 2 * 2:2], mixed[1:number_of // 2 * 2:2]
    room = jnp.minimum(sizes[giver] - 1, most - sizes[taker]) // 2
    room = jnp.where((giver == sequence[0]) | (taker == sequence[0]) | (sizes[taker] == 0), 0, jnp.maximum(room, 0))
    passed = jax.random.randint(jax.random.fold_in(own, 4), (number_of // 2,), 0, 1 << 20) % (room + 1)
    sizes = sizes.at[giver].add(-passed).at[taker].add(passed)
    labels = jnp.searchsorted(jnp.cumsum(sizes), jnp.arange(rows * top), side="right").astype(jnp.int32)
    listing = labels.reshape(top, rows).T
    listing = listing[jax.random.permutation(jax.random.fold_in(own, 1), rows)]
    turn = jax.random.randint(jax.random.fold_in(own, 2), (rows, 1), 0, top)
    return jnp.take_along_axis(listing, (jnp.arange(top)[None, :] + turn) % top, axis=1)


def portions_of(amount, total, limit, slope, full):
    loads = [(1 << 20) // math.isqrt(rank ** slope) + 1 for rank in range(1, amount + 1)]
    largest = limit if full else min(limit, max(-(-total // amount), total * loads[0] // sum(loads)))
    least = 1 if total - largest >= amount - 1 else 0
    counts, surplus = [largest] + [least] * (amount - 1), total - largest - least * (amount - 1)
    while surplus > 0:
        movable = [i for i in range(1, amount) if counts[i] < largest] or [i for i in range(1, amount) if counts[i] < limit]
        mass, budget = sum([loads[i] for i in movable]), surplus
        for i in movable:
            extra = min(limit - counts[i], max(1, budget * loads[i] // mass), surplus)
            counts[i] = counts[i] + extra
            surplus = surplus - extra
    return np.array(counts)


def bell_draw(stream_key, dims, spread, reach, split=(), kind=jnp.bfloat16):
    result = spread * jax.random.normal(stream_key, dims, jnp.float32)
    if split:
        result = result * levels(stream_key, dims, split, -0.22, 0.18)
    return jnp.clip(result, -reach, reach).astype(kind)


def setup_inputs(seed: int = 0) -> dict:
    keys = jax.random.split(jax.random.key(seed), 9)
    state = jnp.clip(jax.random.uniform(keys[0], (NBR, NBC, SEQ, U), jnp.float32, -1.0, 1.0) * levels(keys[0], (NBR, NBC, SEQ, U), ((0, 16), (1, 8)), -0.4, 0.0), -1.0, 1.0).astype(jnp.bfloat16)
    weights = bell_draw(keys[1], (NBR, NBC, STENCIL + LINKS + 1, U, U), ((STENCIL + LINKS + 1) * U) ** -0.5, 0.125, ((0, 16), (1, 8)))
    drive = bell_draw(keys[2], (STEPS, NBR, NBC, SEQ, U), 1.0, 6.0, ((1, 16), (2, 8)))
    leak = jnp.clip(jnp.exp(math.log(1.0) - 2.3025851 * jax.random.uniform(keys[3], (NBR, NBC, U), jnp.float32) ** levels(keys[3], (NBR, NBC, U), ((0, 16), (1, 8)), -0.2, 0.2)), 0.1, 1.0)
    link_dev_keys = jax.random.split(jax.random.fold_in(keys[4], 1), N_GX * N_GY * (R * C) // (R * C))
    link_dev_turns = jax.random.permutation(jax.random.fold_in(keys[4], 3), N_GX * N_GY * (R * C) // (R * C))
    link_dev = jax.vmap(lambda own, number: routed_block(jax.random.fold_in(keys[4], 2), own, number, R * C, N_GX, LINKS, CAP, 2))(link_dev_keys, link_dev_turns).reshape((N_GX, N_GY, R * C, LINKS))
    link_blk = place_ends(jax.random.randint(keys[5], (N_GX, N_GY, R * C, LINKS), 0, R * C), jax.random.fold_in(keys[5], 1), 0, (R * C) - 1).astype(jnp.int32)
    offsets = draw_offsets(jax.random.fold_in(keys[8], 71), 0)
    gram_prev = bell_draw(keys[7], (NBR, NBC, U, U), 1.0, 6.0, ((0, 16), (1, 8)), jnp.float32)
    return dict(state=state, weights=weights, drive=drive, leak=leak, link_dev=link_dev, link_blk=link_blk, offsets=offsets, gram_prev=gram_prev)


def reference(state, weights, drive, leak, link_dev, link_blk, offsets, gram_prev):
    dev_grid = link_dev.reshape(N_GX, N_GY, R, C, LINKS).transpose(0, 2, 1, 3, 4).reshape(NBR, NBC, LINKS)
    blk_grid = link_blk.reshape(N_GX, N_GY, R, C, LINKS).transpose(0, 2, 1, 3, 4).reshape(NBR, NBC, LINKS)
    col_band = (jnp.arange(NBC, dtype=jnp.int32) // C)[None, :, None]
    src_row = (dev_grid * R + blk_grid // C).astype(jnp.int32)
    src_col = (col_band * C + blk_grid % C).astype(jnp.int32)
    current = state
    gram = gram_prev
    for step_id in range(STEPS):
        padded = jnp.pad(current, ((1, 1), (1, 1), (0, 0), (0, 0)))

        def one_row(row_id):
            w_row = lax.dynamic_index_in_dim(weights, row_id, 0, keepdims=False)
            preact = jnp.zeros((NBC, SEQ, U), jnp.float32)
            for offset_id in range(STENCIL):
                start_r = (row_id + 1 + offsets[offset_id, 0]).astype(jnp.int32)
                start_c = (1 + offsets[offset_id, 1]).astype(jnp.int32)
                zero = jnp.zeros((), jnp.int32)
                nearby = lax.dynamic_slice(padded, (start_r, start_c, zero, zero), (1, NBC, SEQ, U))[0]
                preact = preact + jnp.einsum("csu,cuv->csv", nearby.astype(jnp.float32), w_row[:, offset_id].astype(jnp.float32))
            sources = current[src_row[row_id], src_col[row_id]]
            preact = preact + jnp.einsum("clsu,cluv->csv", sources.astype(jnp.float32), w_row[:, STENCIL:STENCIL + LINKS].astype(jnp.float32))
            inputs = lax.dynamic_index_in_dim(drive[step_id], row_id, 0, keepdims=False)
            preact = preact + jnp.einsum("csu,cuv->csv", inputs.astype(jnp.float32), w_row[:, STENCIL + LINKS].astype(jnp.float32))
            old_row = lax.dynamic_index_in_dim(current, row_id, 0, keepdims=False).astype(jnp.float32)
            rate = lax.dynamic_index_in_dim(leak, row_id, 0, keepdims=False)[:, None, :]
            fresh = ((1.0 - rate) * old_row + rate * jnp.tanh(preact)).astype(jnp.bfloat16)
            fresh_wide = fresh.astype(jnp.float32)
            return fresh, jnp.einsum("csu,csv->cuv", fresh_wide, fresh_wide)

        fresh_all, gram_terms = lax.map(one_row, jnp.arange(NBR, dtype=jnp.int32))
        current = fresh_all
        gram = gram + gram_terms
    return current, gram
```

```python
import functools

import jax
import jax.numpy as jnp
from jax import lax
from jax.experimental import pallas as pl
from jax.experimental.pallas import tpu as pltpu
from jax.sharding import Mesh, PartitionSpec as P

VMEM_BYTES = 56 * 1024 * 1024
ANY = pl.BlockSpec(memory_space=pl.ANY)
SMEM = pl.BlockSpec(memory_space=pltpu.SMEM)
VMEM = pl.BlockSpec(memory_space=pltpu.VMEM)
RING = 4


def plan_kernel(dims, pos, dev, blk, offs, send, near, far, count, seen):
    rows, cols, nlinks, nstencil, cap, ngx, ngy = dims
    nblk = rows * cols
    me, band = pos[0], pos[1]
    mine = (me // RING, me % RING)
    dests = [me]
    dests += [((mine[0] + way) % RING) * RING + mine[1] for way in range(1, RING)]
    dests += [mine[0] * RING + (mine[1] + way) % RING for way in range(1, RING)]

    @pl.loop(0, ngx)
    def _(i):
        for n in range(len(dests)):
            seen[n, i] = 0

    for half in range(2):
        for kind in range(2 * RING):
            count[half, kind] = 0
        for way in range(RING - 1):
            for rel in range(RING):
                for i in range(cap):
                    send[half, way, rel, i] = 0

    @pl.loop(0, nblk)
    def _(q):
        for l in range(nlinks):
            for n, dest in enumerate(dests):
                d = dev[dest, 0, q, l]
                at = (d // RING, d % RING)
                i = seen[n, d]
                seen[n, d] = i + 1
                i = jnp.minimum(i, cap - 1)
                if n:
                    half, way = (n - 1) // (RING - 1), (n - 1) % (RING - 1)

                    @pl.when(at[half] == mine[half])
                    def _(half=half, way=way, at=at, i=i, dest=dest):
                        rel = (at[1 - half] - mine[1 - half] + RING) % RING
                        send[half, way, rel, i] = blk[dest, 0, q, l]

                    continue
                for half in range(2):
                    way = (at[half] - mine[half] + RING) % RING
                    rel = (at[1 - half] - mine[1 - half] + RING) % RING
                    own = blk[me, 0, q, l]
                    upper = (rel == RING // 2) & (own >= nblk // 2)
                    kind = jnp.where(way == 0, jnp.where(upper, 2 * RING - 1, rel), RING + way - 1)
                    place = jnp.where(way == 0, jnp.where(upper, own - nblk // 2, own), rel * cap + i)
                    k = count[half, kind]
                    far[half, kind, jnp.minimum(k, RING * cap - 1)] = place * 64 + q * nlinks + l
                    count[half, kind] = k + 1

    side = nblk + 2 * cols
    swap = band % 2
    left, right = side + (1 - swap) * (rows + 2), side + swap * (rows + 2)
    void = side + 2 * (rows + 2)

    @pl.loop(0, rows)
    def _(r0):
        for c0 in range(cols):
            for k in range(nstencil):
                r, t = r0 + offs[k, 0], c0 + offs[k, 1]
                code = jnp.where(r < 0, nblk + t, jnp.where(r >= rows, nblk + cols + t, r * cols + t))
                code = jnp.where(t < 0, left + r + 1, jnp.where(t >= cols, right + r + 1, code))
                out = (r < 0) & (me == 0) | (r >= rows) & (me == ngx - 1)
                out = out | (t < 0) & (band == 0) | (t >= cols) & (band == ngy - 1)
                near[(r0 * cols + c0) * nstencil + k] = jnp.where(out, void, code)


def pack_kernel(cap, send, *refs):
    nsrc, nout = 2 * (RING + 1), 2 * (RING - 1)
    srcs, outs = refs[:nsrc], refs[nsrc : nsrc + nout]
    pool, slots, sem, osem = refs[nsrc + nout :]
    loads, at = [], 0
    for i, src in enumerate(srcs):
        half = i // (RING + 1)
        at = 0 if i % (RING + 1) == 0 else at
        n = src.shape[0]
        loads.append(pltpu.make_async_copy(src, pool.at[half, pl.ds(at, n)], sem.at[i]))
        at += n
    for c in loads:
        c.start()
    nblk = srcs[0].shape[0]
    puts = []
    for half in range(2):
        for c in loads[half * (RING + 1) : (half + 1) * (RING + 1)]:
            c.wait()
        for way in range(RING - 1):
            n = half * (RING - 1) + way
            for rel in range(RING):
                for i in range(cap):
                    slots[n, rel * cap + i] = pool[half, rel * nblk + send[half, way, rel, i]]
            puts.append(pltpu.make_async_copy(slots.at[n], outs[n], osem.at[n]))
            puts[-1].start()
    for c in puts:
        c.wait()


def near_kernel(dims, nrim, grams, t, near, own_ref, *refs):
    nblk, nstencil, nsrc = dims
    rims, refs = refs[: len(nrim)], list(refs[len(nrim) :])
    w_ref, drive_ref = refs[:2]
    refs = refs[2:]
    gram_ref = refs.pop(0) if grams else None
    pre_ref = refs.pop(0)
    gram_out = refs.pop(0) if grams else None
    pool, wst, wdr, dr, pre, *refs = refs
    gin, gout = (refs.pop(0), refs.pop(0)) if grams else (None, None)
    sem, osem = refs
    units = own_ref.shape[-1]
    copies, at = [pltpu.make_async_copy(own_ref, pool.at[pl.ds(0, nblk)], sem.at[nblk])], nblk
    for i, n in enumerate(nrim):
        copies.append(pltpu.make_async_copy(rims[i], pool.at[pl.ds(at, n)], sem.at[nblk + i + 1]))
        at += n

    def ins(q):
        yield pltpu.make_async_copy(w_ref.at[q, pl.ds(0, nstencil)], wst.at[q], sem.at[q])
        yield pltpu.make_async_copy(w_ref.at[q, nsrc], wdr.at[q], sem.at[q])
        yield pltpu.make_async_copy(drive_ref.at[t, q], dr.at[q], sem.at[q])
        if grams:
            yield pltpu.make_async_copy(gram_ref.at[q], gin.at[q], sem.at[q])

    def puts(q):
        yield pltpu.make_async_copy(pre.at[q], pre_ref.at[q], osem.at[q])
        if grams:
            yield pltpu.make_async_copy(gout.at[q], gram_out.at[q], osem.at[q])

    for c in copies:
        c.start()

    @pl.loop(0, nblk)
    def _(q):
        for c in ins(q):
            c.start()

    pool[at] = jnp.zeros_like(pool[at])
    for c in copies:
        c.wait()

    @pl.loop(0, nblk)
    def _(q):
        for c in ins(q):
            c.wait()
        lhs = jnp.concatenate([pool[near[q * nstencil + k]] for k in range(nstencil)] + [dr[q]], axis=1)
        w = jnp.concatenate([wst[q].reshape(nstencil * units, units), wdr[q]], axis=0)
        pre[q] = jnp.dot(lhs, w, preferred_element_type=jnp.float32)
        if grams:
            x = pool[q]
            gout[q] = gin[q] + lax.dot_general(x, x, (((0,), (0,)), ((), ())), preferred_element_type=jnp.float32)
        for c in puts(q):
            c.start()

    @pl.loop(0, nblk)
    def _(q):
        for c in puts(q):
            c.wait()


def far_kernel(dims, last, far, count, *refs):
    nblk, h, nstencil, nlinks = dims
    nin = 4 * RING
    bufs, refs = refs[:nin], list(refs[nin:])
    own_ref, w_ref, pre_ref, leak_ref = refs[:4]
    refs = refs[4:]
    gram_ref = refs.pop(0) if last else None
    nout = 2 if last else 3
    outs, refs = refs[:nout], refs[nout:]
    got, old, wl, pre, new, *refs = refs
    gin, gout = (refs.pop(0), refs.pop(0)) if last else (None, None)
    sem, osem = refs

    for half in range(2):
        for kind in range(2 * RING):
            src = bufs[half * 2 * RING + kind]

            @pl.loop(0, count[half, kind])
            def _(n, half=half, kind=kind, src=src):
                e = far[half, kind, n]
                to = got.at[e % 64, pl.ds(half * h, h)]
                pltpu.make_async_copy(src.at[e // 64], to, sem.at[nblk]).start()

    def ins(q):
        yield pltpu.make_async_copy(own_ref.at[q], old.at[q], sem.at[q])
        yield pltpu.make_async_copy(w_ref.at[q, pl.ds(nstencil, nlinks)], wl.at[q], sem.at[q])
        yield pltpu.make_async_copy(pre_ref.at[q], pre.at[q], sem.at[q])
        if last:
            yield pltpu.make_async_copy(gram_ref.at[q], gin.at[q], sem.at[q])

    def puts(q):
        if last:
            yield pltpu.make_async_copy(new.at[q], outs[0].at[q], osem.at[q])
            yield pltpu.make_async_copy(gout.at[q], outs[1].at[q], osem.at[q])
        else:
            yield pltpu.make_async_copy(new.at[q, pl.ds(0, h)], outs[0].at[q], osem.at[q])
            yield pltpu.make_async_copy(new.at[q, pl.ds(h, h)], outs[1].at[q], osem.at[q])
            yield pltpu.make_async_copy(new.at[q], outs[2].at[q], osem.at[q])

    @pl.loop(0, nblk)
    def _(q):
        for c in ins(q):
            c.start()

    pltpu.make_async_copy(got, got, sem.at[nblk]).wait()

    @pl.loop(0, nblk)
    def _(q):
        for c in ins(q):
            c.wait()
        lhs = jnp.concatenate([got[q * nlinks + l] for l in range(nlinks)], axis=1)
        units = lhs.shape[-1] // nlinks
        w = wl[q].reshape(nlinks * units, units)
        total = pre[q] + jnp.dot(lhs, w, preferred_element_type=jnp.float32)
        rate = leak_ref[pl.ds(q, 1), :]
        fresh = ((1.0 - rate) * old[q].astype(jnp.float32) + rate * jnp.tanh(total)).astype(jnp.bfloat16)
        new[q] = fresh
        if last:
            gout[q] = gin[q] + lax.dot_general(
                fresh, fresh, (((0,), (0,)), ((), ())), preferred_element_type=jnp.float32
            )
        for c in puts(q):
            c.start()

    @pl.loop(0, nblk)
    def _(q):
        for c in puts(q):
            c.wait()


def after(x, *done):
    return lax.optimization_barrier((x, *done))[0]


def shards(state, weights, drive, leak, link_dev, link_blk, offsets, gram_prev):
    rows, cols, seq, units = state.shape
    nblk = rows * cols
    nlinks = link_dev.shape[-1]
    nstencil = offsets.shape[0]
    ngx = RING * RING
    cap = 4
    slots = RING * cap
    steps = drive.shape[0]
    gx = ("x", "y")
    gy = ("z", "core")
    ny = lax.axis_size(gy)
    nsrc = nstencil + nlinks
    bf16 = jnp.bfloat16
    f32 = jnp.float32
    h = seq // 2
    params = pltpu.CompilerParams(vmem_limit_bytes=VMEM_BYTES)
    kinds = 2 * RING
    pos = jnp.stack([lax.axis_index(gx), lax.axis_index(gy)]).astype(jnp.int32)
    send, near, far, count = pl.pallas_call(
        functools.partial(plan_kernel, (rows, cols, nlinks, nstencil, cap, ngx, ny)),
        out_shape=(
            jax.ShapeDtypeStruct((2, RING - 1, RING, cap), jnp.int32),
            jax.ShapeDtypeStruct((nblk * nstencil,), jnp.int32),
            jax.ShapeDtypeStruct((2, kinds, slots), jnp.int32),
            jax.ShapeDtypeStruct((2, kinds), jnp.int32),
        ),
        in_specs=[SMEM] * 4,
        out_specs=(SMEM,) * 4,
        scratch_shapes=[pltpu.SMEM((2 * RING - 1, ngx), jnp.int32)],
        name="plan",
    )(pos, link_dev, link_blk, offsets)

    state = state.reshape(nblk, seq, units)
    weights = weights.reshape(nblk, nsrc + 1, units, units)
    drive = drive.reshape(steps, nblk, seq, units)
    leak = leak.reshape(nblk, units)
    gram = gram_prev.reshape(nblk, units, units)

    def shift(x, axis, k):
        return lax.ppermute(x, axis, [(i, (i - k) % RING) for i in range(RING)])

    def ring(x, k):
        return lax.ppermute(x, gx, [(i, (i + k) % ngx) for i in range(ngx)])

    def first(a, b, full):
        grid = full.reshape(rows, cols, seq, units)
        above, below = ring(grid[rows - 1], 1), ring(grid[0], -1)
        a1 = after(a, above, below)
        y1, y3 = shift(a1, "y", 1), shift(a1, "y", 3)
        x1, x3 = shift(b, "x", 1), shift(b, "x", 3)
        m = nblk // 2
        y2l, y2u = shift(y1[:m], "y", 1), shift(y3[m:], "y", 3)
        x2l, x2u = shift(x1[:m], "x", 1), shift(x3[m:], "x", 3)
        return [a, y1, y2l, y2u, y3], [b, x1, x2l, x2u, x3], above, below

    def pack(a, b):
        return pl.pallas_call(
            functools.partial(pack_kernel, cap),
            out_shape=[jax.ShapeDtypeStruct((slots, h, units), bf16)] * (2 * (RING - 1)),
            in_specs=[SMEM] + [ANY] * (len(a) + len(b)),
            out_specs=[ANY] * (2 * (RING - 1)),
            scratch_shapes=[
                pltpu.VMEM((2, RING * nblk, h, units), bf16),
                pltpu.VMEM((2 * (RING - 1), slots, h, units), bf16),
                pltpu.SemaphoreType.DMA((len(a) + len(b),)),
                pltpu.SemaphoreType.DMA((2 * (RING - 1),)),
            ],
            compiler_params=params,
            name="pack",
        )(send, *a, *b)

    def second(packed, full, above, below):
        pa, pb = packed[: RING - 1], packed[RING - 1 :]
        x1, x3 = shift(pa[2], "x", 1), shift(pa[0], "x", 3)
        y1, y3 = shift(pb[2], "y", 1), shift(pb[0], "y", 3)
        done = (x1, x3, y1, y3)
        x2, y2 = shift(after(pa[1], *done), "x", 2), shift(after(pb[1], *done), "y", 2)
        grid = full.reshape(rows, cols, seq, units)
        tall = lambda c: jnp.concatenate([above[c : c + 1], grid[:, c], below[c : c + 1]], axis=0)
        even = lax.axis_index("core") == 0
        chip, step = jnp.where(even, tall(cols - 1), tall(0)), jnp.where(even, tall(0), tall(cols - 1))
        core = lax.ppermute(after(chip, *done), gy, [(i, i + 1 - 2 * (i % 2)) for i in range(ny)])
        side = lax.ppermute(after(step, *done), gy, [(i, (i - 1 + 2 * (i % 2)) % ny) for i in range(ny)])
        return [x1, x2, x3], [y1, y2, y3], [above, below, core, side]

    def products(t, full, rim, gram):
        nrim = tuple(r.shape[0] for r in rim)
        args = [near, full, *rim, weights, drive]
        outs = [jax.ShapeDtypeStruct((nblk, seq, units), f32)]
        scratch = [
            pltpu.VMEM((nblk + sum(nrim) + 1, seq, units), bf16),
            pltpu.VMEM((nblk, nstencil, units, units), bf16),
            pltpu.VMEM((nblk, units, units), bf16),
            pltpu.VMEM((nblk, seq, units), bf16),
            pltpu.VMEM((nblk, seq, units), f32),
        ]
        if gram is not None:
            args.append(gram)
            outs.append(jax.ShapeDtypeStruct((nblk, units, units), f32))
            scratch += [pltpu.VMEM((nblk, units, units), f32)] * 2
        scratch += [pltpu.SemaphoreType.DMA((nblk + 1 + len(nrim),)), pltpu.SemaphoreType.DMA((nblk,))]
        return pl.pallas_call(
            functools.partial(near_kernel, (nblk, nstencil, nsrc), nrim, gram is not None, t),
            out_shape=outs,
            in_specs=[SMEM] + [ANY] * (len(args) - 1),
            out_specs=[ANY] * len(outs),
            scratch_shapes=scratch,
            compiler_params=params,
            name="near",
        )(*args)

    def finish(a, b, ga, gb, full, pre, gram, last):
        args = [far, count]
        for x, g in ((a, ga), (b, gb)):
            args += [*x[:3], x[4], *g, x[3]]
        args += [full, weights, pre, leak]
        in_specs = [SMEM] * 2 + [ANY] * (len(args) - 3) + [VMEM]
        scratch = [
            pltpu.VMEM((nblk * nlinks, seq, units), bf16),
            pltpu.VMEM((nblk, seq, units), bf16),
            pltpu.VMEM((nblk, nlinks, units, units), bf16),
            pltpu.VMEM((nblk, seq, units), f32),
            pltpu.VMEM((nblk, seq, units), bf16),
        ]
        if last:
            args.append(gram)
            in_specs.append(ANY)
            outs = [jax.ShapeDtypeStruct((nblk, seq, units), bf16), jax.ShapeDtypeStruct((nblk, units, units), f32)]
            scratch += [pltpu.VMEM((nblk, units, units), f32)] * 2
        else:
            outs = [jax.ShapeDtypeStruct((nblk, n, units), bf16) for n in (h, h, seq)]
        scratch += [pltpu.SemaphoreType.DMA((nblk + 1,)), pltpu.SemaphoreType.DMA((nblk,))]
        return pl.pallas_call(
            functools.partial(far_kernel, (nblk, h, nstencil, nlinks), last),
            out_shape=outs,
            in_specs=in_specs,
            out_specs=[ANY] * len(outs),
            scratch_shapes=scratch,
            compiler_params=params,
            name="far",
        )(*args)

    own_a, own_b, full = state[:, :h], state[:, h:], state
    for t in range(steps):
        a, b, above, below = first(own_a, own_b, full)
        packed = pack(a, b)
        ga, gb, rim = second(packed, full, above, below)
        res = products(t, full, rim, gram if t else None)
        pre = res[0]
        if t:
            gram = res[1]
        res = finish(a, b, ga, gb, full, pre, gram, t == steps - 1)
        if t < steps - 1:
            own_a, own_b, full = res
    final, gram = res
    return final.reshape(rows, cols, seq, units), gram.reshape(rows, cols, units, units)


def solution(mesh):
    grid = Mesh(mesh.devices.reshape(4, 4, 4, 2), ("x", "y", "z", "core"))
    gx, gy = ("x", "y"), ("z", "core")
    return jax.shard_map(
        shards,
        mesh=grid,
        in_specs=(
            P(gx, gy, None, None),
            P(gx, gy, None, None, None),
            P(None, gx, gy, None, None),
            P(gx, gy, None),
            P(None, gy, None, None),
            P(None, gy, None, None),
            P(),
            P(gx, gy, None, None),
        ),
        out_specs=(P(gx, gy, None, None), P(gx, gy, None, None)),
        check_vma=False,
    )
```

```python
import functools

import jax
import jax.numpy as jnp
from jax import lax
from jax.experimental import pallas as pl
from jax.experimental.pallas import tpu as pltpu
from jax.sharding import Mesh, PartitionSpec as P

VMEM_BYTES = 56 * 1024 * 1024
ANY = pl.BlockSpec(memory_space=pl.ANY)
SMEM = pl.BlockSpec(memory_space=pltpu.SMEM)
VMEM = pl.BlockSpec(memory_space=pltpu.VMEM)
RING = 4
BITS, MASK = 2, RING - 1


def plan_kernel(dims, pos, dev, blk, offs, send, near, far, count, beside, nbeside, seen):
    rows, cols, nlinks, nstencil, cap, ngx, ngy = dims
    nblk = rows * cols
    me, band = pos[0], pos[1]
    mine = (me >> BITS, me & MASK)
    dests = [me]
    dests += [((mine[0] + way) & MASK) * RING + mine[1] for way in range(1, RING)]
    dests += [mine[0] * RING + ((mine[1] + way) & MASK) for way in range(1, RING)]

    @pl.loop(0, ngx)
    def _(i):
        for n in range(len(dests)):
            seen[n, i] = 0

    for half in range(2):
        for kind in range(2 * RING):
            count[half, kind] = 0
        for way in range(RING - 1):
            for rel in range(RING):
                for i in range(cap):
                    send[half, way, rel, i] = 0

    @pl.loop(0, nblk)
    def _(q):
        for l in range(nlinks):
            for n, dest in enumerate(dests):
                d = dev[dest, 0, q, l]
                at = (d >> BITS, d & MASK)
                i = seen[n, d]
                seen[n, d] = i + 1
                i = jnp.minimum(i, cap - 1)
                if n:
                    half, way = (n - 1) // (RING - 1), (n - 1) % (RING - 1)

                    @pl.when(at[half] == mine[half])
                    def _(half=half, way=way, at=at, i=i, dest=dest):
                        rel = (at[1 - half] - mine[1 - half]) & MASK
                        send[half, way, rel, i] = blk[dest, 0, q, l]

                    continue
                for half in range(2):
                    way = (at[half] - mine[half]) & MASK
                    rel = (at[1 - half] - mine[1 - half]) & MASK
                    own = blk[me, 0, q, l]
                    upper = (rel == RING // 2) & (own >= nblk // 2)
                    kind = jnp.where(way == 0, jnp.where(upper, 2 * RING - 1, rel), RING + way - 1)
                    place = jnp.where(way == 0, jnp.where(upper, own - nblk // 2, own), rel * cap + i)
                    k = count[half, kind]
                    far[half, kind, jnp.minimum(k, RING * cap - 1)] = place * 64 + q * nlinks + l
                    count[half, kind] = k + 1

    swap = band & 1
    void = nblk + 2 * cols
    nbeside[0] = 0

    @pl.loop(0, rows)
    def _(r0):
        for c0 in range(cols):
            for k in range(nstencil):
                r, t = r0 + offs[k, 0], c0 + offs[k, 1]
                code = jnp.where(r < 0, nblk + t, jnp.where(r >= rows, nblk + cols + t, r * cols + t))
                out = (r < 0) & (me == 0) | (r >= rows) & (me == ngx - 1)
                left, right = t < 0, t >= cols
                term = (r0 * cols + c0) * nstencil + k
                near[term] = jnp.where(out | left | right, void, code)
                if c0 in (0, cols - 1):
                    out = out | left & (band == 0) | right & (band == ngy - 1)

                    @pl.when((left | right) & jnp.logical_not(out))
                    def _(left=left, r=r, c0=c0, k=k):
                        n = nbeside[0]
                        which = jnp.where(left, 1 - swap, swap)
                        beside[n] = (((r0 * cols + c0) * 8 + k) * 64) + which * (rows + 2) + r + 1
                        nbeside[0] = n + 1


def pack_kernel(cap, send, *refs):
    nsrc, nout = 2 * (RING + 1), 2 * (RING - 1)
    srcs, outs = refs[:nsrc], refs[nsrc : nsrc + nout]
    pool, slots, sem, osem = refs[nsrc + nout :]
    loads, at = [], 0
    for i, src in enumerate(srcs):
        half = i // (RING + 1)
        at = 0 if i % (RING + 1) == 0 else at
        n = src.shape[0]
        loads.append(pltpu.make_async_copy(src, pool.at[half, pl.ds(at, n)], sem.at[i]))
        at += n
    for c in loads:
        c.start()
    nblk = srcs[0].shape[0]
    puts = []
    for half in range(2):
        for c in loads[half * (RING + 1) : (half + 1) * (RING + 1)]:
            c.wait()
        for way in range(RING - 1):
            n = half * (RING - 1) + way
            for rel in range(RING):
                for i in range(cap):
                    slots[n, rel * cap + i] = pool[half, rel * nblk + send[half, way, rel, i]]
            puts.append(pltpu.make_async_copy(slots.at[n], outs[n], osem.at[n]))
            puts[-1].start()
    for c in puts:
        c.wait()


def near_kernel(dims, nrim, grams, t, near, own_ref, *refs):
    nblk, nstencil, nsrc = dims
    rims, refs = refs[: len(nrim)], list(refs[len(nrim) :])
    w_ref, drive_ref = refs[:2]
    refs = refs[2:]
    gram_ref = refs.pop(0) if grams else None
    pre_ref = refs.pop(0)
    gram_out = refs.pop(0) if grams else None
    pool, wst, wdr, dr, pre, *refs = refs
    gin, gout = (refs.pop(0), refs.pop(0)) if grams else (None, None)
    sem, osem = refs
    units = own_ref.shape[-1]
    copies, at = [pltpu.make_async_copy(own_ref, pool.at[pl.ds(0, nblk)], sem.at[nblk])], nblk
    for i, n in enumerate(nrim):
        copies.append(pltpu.make_async_copy(rims[i], pool.at[pl.ds(at, n)], sem.at[nblk + i + 1]))
        at += n

    def ins(q):
        yield pltpu.make_async_copy(w_ref.at[q, pl.ds(0, nstencil)], wst.at[q], sem.at[q])
        yield pltpu.make_async_copy(w_ref.at[q, nsrc], wdr.at[q], sem.at[q])
        yield pltpu.make_async_copy(drive_ref.at[t, q], dr.at[q], sem.at[q])
        if grams:
            yield pltpu.make_async_copy(gram_ref.at[q], gin.at[q], sem.at[q])

    def puts(q):
        yield pltpu.make_async_copy(pre.at[q], pre_ref.at[q], osem.at[q])
        if grams:
            yield pltpu.make_async_copy(gout.at[q], gram_out.at[q], osem.at[q])

    for c in copies:
        c.start()

    @pl.loop(0, nblk)
    def _(q):
        for c in ins(q):
            c.start()

    pool[at] = jnp.zeros_like(pool[at])
    for c in copies:
        c.wait()

    @pl.loop(0, nblk)
    def _(q):
        for c in ins(q):
            c.wait()
        lhs = jnp.concatenate([pool[near[q * nstencil + k]] for k in range(nstencil)] + [dr[q]], axis=1)
        w = jnp.concatenate([wst[q].reshape(nstencil * units, units), wdr[q]], axis=0)
        pre[q] = jnp.dot(lhs, w, preferred_element_type=jnp.float32)
        if grams:
            x = pool[q]
            gout[q] = gin[q] + lax.dot_general(x, x, (((0,), (0,)), ((), ())), preferred_element_type=jnp.float32)
        for c in puts(q):
            c.start()

    @pl.loop(0, nblk)
    def _(q):
        for c in puts(q):
            c.wait()


def far_kernel(dims, last, far, count, beside, nbeside, *refs):
    nblk, h, nstencil, nlinks = dims
    nin = 4 * RING
    bufs, refs = refs[:nin], list(refs[nin:])
    core_ref, side_ref, own_ref, w_ref, pre_ref, leak_ref = refs[:6]
    refs = refs[6:]
    gram_ref = refs.pop(0) if last else None
    nout = 2 if last else 3
    outs, refs = refs[:nout], refs[nout:]
    got, cols, wb, old, wl, pre, new, *refs = refs
    gin, gout = (refs.pop(0), refs.pop(0)) if last else (None, None)
    sem, osem, bsem = refs
    tall = core_ref.shape[0]
    whole = [
        pltpu.make_async_copy(pre_ref, pre, sem.at[nblk + 1]),
        pltpu.make_async_copy(core_ref, cols.at[pl.ds(0, tall)], sem.at[nblk + 2]),
        pltpu.make_async_copy(side_ref, cols.at[pl.ds(tall, tall)], sem.at[nblk + 3]),
    ]
    for c in whole:
        c.start()

    def weight(n):
        e = beside[n]
        return pltpu.make_async_copy(w_ref.at[e >> 9, (e >> 6) & 7], wb.at[n], bsem.at[n])

    @pl.loop(0, nbeside[0])
    def _(n):
        weight(n).start()

    for half in range(2):
        for kind in range(2 * RING):
            src = bufs[half * 2 * RING + kind]

            @pl.loop(0, count[half, kind])
            def _(n, half=half, kind=kind, src=src):
                e = far[half, kind, n]
                to = got.at[e & 63, pl.ds(half * h, h)]
                pltpu.make_async_copy(src.at[e >> 6], to, sem.at[nblk]).start()

    def ins(q):
        yield pltpu.make_async_copy(own_ref.at[q], old.at[q], sem.at[q])
        yield pltpu.make_async_copy(w_ref.at[q, pl.ds(nstencil, nlinks)], wl.at[q], sem.at[q])
        if last:
            yield pltpu.make_async_copy(gram_ref.at[q], gin.at[q], sem.at[q])

    def puts(q):
        if last:
            yield pltpu.make_async_copy(new.at[q], outs[0].at[q], osem.at[q])
            yield pltpu.make_async_copy(gout.at[q], outs[1].at[q], osem.at[q])
        else:
            yield pltpu.make_async_copy(new.at[q, pl.ds(0, h)], outs[0].at[q], osem.at[q])
            yield pltpu.make_async_copy(new.at[q, pl.ds(h, h)], outs[1].at[q], osem.at[q])
            yield pltpu.make_async_copy(new.at[q], outs[2].at[q], osem.at[q])

    @pl.loop(0, nblk)
    def _(q):
        for c in ins(q):
            c.start()

    for c in whole:
        c.wait()

    @pl.loop(0, nbeside[0])
    def _(n):
        weight(n).wait()
        e = beside[n]
        pre[e >> 9] += jnp.dot(cols[e & 63], wb[n], preferred_element_type=jnp.float32)

    pltpu.make_async_copy(got, got, sem.at[nblk]).wait()

    @pl.loop(0, nblk)
    def _(q):
        for c in ins(q):
            c.wait()
        lhs = jnp.concatenate([got[q * nlinks + l] for l in range(nlinks)], axis=1)
        units = lhs.shape[-1] // nlinks
        w = wl[q].reshape(nlinks * units, units)
        total = pre[q] + jnp.dot(lhs, w, preferred_element_type=jnp.float32)
        rate = leak_ref[pl.ds(q, 1), :]
        fresh = ((1.0 - rate) * old[q].astype(jnp.float32) + rate * jnp.tanh(total)).astype(jnp.bfloat16)
        new[q] = fresh
        if last:
            gout[q] = gin[q] + lax.dot_general(
                fresh, fresh, (((0,), (0,)), ((), ())), preferred_element_type=jnp.float32
            )
        for c in puts(q):
            c.start()

    @pl.loop(0, nblk)
    def _(q):
        for c in puts(q):
            c.wait()


def after(x, *done):
    return lax.optimization_barrier((x, *done))[0]


def shards(state, weights, drive, leak, link_dev, link_blk, offsets, gram_prev):
    rows, cols, seq, units = state.shape
    nblk = rows * cols
    nlinks = link_dev.shape[-1]
    nstencil = offsets.shape[0]
    ngx = RING * RING
    cap = 4
    slots = RING * cap
    steps = drive.shape[0]
    gx = ("x", "y")
    gy = ("z", "core")
    ny = lax.axis_size(gy)
    nsrc = nstencil + nlinks
    bf16 = jnp.bfloat16
    f32 = jnp.float32
    h = seq // 2
    params = pltpu.CompilerParams(vmem_limit_bytes=VMEM_BYTES)
    kinds = 2 * RING
    pos = jnp.stack([lax.axis_index(gx), lax.axis_index(gy)]).astype(jnp.int32)
    send, near, far, count, beside, nbeside = pl.pallas_call(
        functools.partial(plan_kernel, (rows, cols, nlinks, nstencil, cap, ngx, ny)),
        out_shape=(
            jax.ShapeDtypeStruct((2, RING - 1, RING, cap), jnp.int32),
            jax.ShapeDtypeStruct((nblk * nstencil,), jnp.int32),
            jax.ShapeDtypeStruct((2, kinds, slots), jnp.int32),
            jax.ShapeDtypeStruct((2, kinds), jnp.int32),
            jax.ShapeDtypeStruct((rows * nstencil,), jnp.int32),
            jax.ShapeDtypeStruct((1,), jnp.int32),
        ),
        in_specs=[SMEM] * 4,
        out_specs=(SMEM,) * 6,
        scratch_shapes=[pltpu.SMEM((2 * RING - 1, ngx), jnp.int32)],
        name="plan",
    )(pos, link_dev, link_blk, offsets)

    state = state.reshape(nblk, seq, units)
    weights = weights.reshape(nblk, nsrc + 1, units, units)
    drive = drive.reshape(steps, nblk, seq, units)
    leak = leak.reshape(nblk, units)
    gram = gram_prev.reshape(nblk, units, units)

    def shift(x, axis, k):
        return lax.ppermute(x, axis, [(i, (i - k) % RING) for i in range(RING)])

    def ring(x, k):
        return lax.ppermute(x, gx, [(i, (i + k) % ngx) for i in range(ngx)])

    def first(a, b, full):
        grid = full.reshape(rows, cols, seq, units)
        y1, y3 = shift(a, "y", 1), shift(a, "y", 3)
        x1, x3 = shift(b, "x", 1), shift(b, "x", 3)
        m = nblk // 2
        done = (y1, y3, x1, x3, count)
        y2l, y2u = shift(after(y1[:m], *done), "y", 1), shift(after(y3[m:], *done), "y", 3)
        x2l, x2u = shift(after(x1[:m], *done), "x", 1), shift(after(x3[m:], *done), "x", 3)
        above, below = ring(after(grid[rows - 1], *done), 1), ring(after(grid[0], *done), -1)
        a = [after(a, above, below), y1, y2l, y2u, y3]
        return a, [b, x1, x2l, x2u, x3], above, below

    def pack(a, b):
        return pl.pallas_call(
            functools.partial(pack_kernel, cap),
            out_shape=[jax.ShapeDtypeStruct((slots, h, units), bf16)] * (2 * (RING - 1)),
            in_specs=[SMEM] + [ANY] * (len(a) + len(b)),
            out_specs=[ANY] * (2 * (RING - 1)),
            scratch_shapes=[
                pltpu.VMEM((2, RING * nblk, h, units), bf16),
                pltpu.VMEM((2 * (RING - 1), slots, h, units), bf16),
                pltpu.SemaphoreType.DMA((len(a) + len(b),)),
                pltpu.SemaphoreType.DMA((2 * (RING - 1),)),
            ],
            compiler_params=params,
            name="pack",
        )(send, *a, *b)

    def second(packed, full, above, below):
        pa, pb = packed[: RING - 1], packed[RING - 1 :]
        x1, x3 = shift(pa[2], "x", 1), shift(pa[0], "x", 3)
        y1, y3 = shift(pb[2], "y", 1), shift(pb[0], "y", 3)
        done = (x1, x3, y1, y3)
        x2, y2 = shift(after(pa[1], *done), "x", 2), shift(after(pb[1], *done), "y", 2)
        grid = full.reshape(rows, cols, seq, units)
        tall = lambda c: jnp.concatenate([above[c : c + 1], grid[:, c], below[c : c + 1]], axis=0)
        even = lax.axis_index("core") == 0
        chip, step = jnp.where(even, tall(cols - 1), tall(0)), jnp.where(even, tall(0), tall(cols - 1))
        core = lax.ppermute(after(chip, *done), gy, [(i, i + 1 - 2 * (i % 2)) for i in range(ny)])
        side = lax.ppermute(after(step, *done), gy, [(i, (i - 1 + 2 * (i % 2)) % ny) for i in range(ny)])
        return [x1, x2, x3], [y1, y2, y3], core, side

    def products(t, full, rim, gram):
        nrim = tuple(r.shape[0] for r in rim)
        args = [near, full, *rim, weights, drive]
        outs = [jax.ShapeDtypeStruct((nblk, seq, units), f32)]
        scratch = [
            pltpu.VMEM((nblk + sum(nrim) + 1, seq, units), bf16),
            pltpu.VMEM((nblk, nstencil, units, units), bf16),
            pltpu.VMEM((nblk, units, units), bf16),
            pltpu.VMEM((nblk, seq, units), bf16),
            pltpu.VMEM((nblk, seq, units), f32),
        ]
        if gram is not None:
            args.append(gram)
            outs.append(jax.ShapeDtypeStruct((nblk, units, units), f32))
            scratch += [pltpu.VMEM((nblk, units, units), f32)] * 2
        scratch += [pltpu.SemaphoreType.DMA((nblk + 1 + len(nrim),)), pltpu.SemaphoreType.DMA((nblk,))]
        return pl.pallas_call(
            functools.partial(near_kernel, (nblk, nstencil, nsrc), nrim, gram is not None, t),
            out_shape=outs,
            in_specs=[SMEM] + [ANY] * (len(args) - 1),
            out_specs=[ANY] * len(outs),
            scratch_shapes=scratch,
            compiler_params=params,
            name="near",
        )(*args)

    def finish(a, b, ga, gb, core, side, full, pre, gram, last):
        args = [far, count, beside, nbeside]
        for x, g in ((a, ga), (b, gb)):
            args += [*x[:3], x[4], *g, x[3]]
        args += [core, side, full, weights, pre, leak]
        in_specs = [SMEM] * 4 + [ANY] * (len(args) - 5) + [VMEM]
        scratch = [
            pltpu.VMEM((nblk * nlinks, seq, units), bf16),
            pltpu.VMEM((2 * (rows + 2), seq, units), bf16),
            pltpu.VMEM((rows * nstencil, units, units), bf16),
            pltpu.VMEM((nblk, seq, units), bf16),
            pltpu.VMEM((nblk, nlinks, units, units), bf16),
            pltpu.VMEM((nblk, seq, units), f32),
            pltpu.VMEM((nblk, seq, units), bf16),
        ]
        if last:
            args.append(gram)
            in_specs.append(ANY)
            outs = [jax.ShapeDtypeStruct((nblk, seq, units), bf16), jax.ShapeDtypeStruct((nblk, units, units), f32)]
            scratch += [pltpu.VMEM((nblk, units, units), f32)] * 2
        else:
            outs = [jax.ShapeDtypeStruct((nblk, n, units), bf16) for n in (h, h, seq)]
        scratch += [pltpu.SemaphoreType.DMA((n,)) for n in (nblk + 4, nblk, rows * nstencil)]
        return pl.pallas_call(
            functools.partial(far_kernel, (nblk, h, nstencil, nlinks), last),
            out_shape=outs,
            in_specs=in_specs,
            out_specs=[ANY] * len(outs),
            scratch_shapes=scratch,
            compiler_params=params,
            name="far",
        )(*args)

    own_a, own_b, full = state[:, :h], state[:, h:], state
    for t in range(steps):
        a, b, above, below = first(own_a, own_b, full)
        packed = pack(a, b)
        ga, gb, core, side = second(packed, full, above, below)
        res = products(t, after(full, packed[0]), [above, below], gram if t else None)
        pre = res[0]
        if t:
            gram = res[1]
        res = finish(a, b, ga, gb, core, side, full, pre, gram, t == steps - 1)
        if t < steps - 1:
            own_a, own_b, full = res
    final, gram = res
    return final.reshape(rows, cols, seq, units), gram.reshape(rows, cols, units, units)


def solution(mesh):
    grid = Mesh(mesh.devices.reshape(4, 4, 4, 2), ("x", "y", "z", "core"))
    gx, gy = ("x", "y"), ("z", "core")
    return jax.shard_map(
        shards,
        mesh=grid,
        in_specs=(
            P(gx, gy, None, None),
            P(gx, gy, None, None, None),
            P(None, gx, gy, None, None),
            P(gx, gy, None),
            P(None, gy, None, None),
            P(None, gy, None, None),
            P(),
            P(gx, gy, None, None),
        ),
        out_specs=(P(gx, gy, None, None), P(gx, gy, None, None)),
        check_vma=False,
    )
```

```python
import functools

import jax
import jax.numpy as jnp
from jax import lax
from jax.experimental import pallas as pl
from jax.experimental.pallas import tpu as pltpu
from jax.sharding import Mesh, PartitionSpec as P

VMEM_BYTES = 56 * 1024 * 1024
ANY = pl.BlockSpec(memory_space=pl.ANY)
SMEM = pl.BlockSpec(memory_space=pltpu.SMEM)
VMEM = pl.BlockSpec(memory_space=pltpu.VMEM)
RING = 4
BITS, MASK = 2, RING - 1


def plan_kernel(dims, pos, dev, blk, offs, send, near, far, count, beside, nbeside, seen):
    rows, cols, nlinks, nstencil, cap, ngx, ngy = dims
    nblk = rows * cols
    me, band = pos[0], pos[1]
    mine = (me >> BITS, me & MASK)
    dests = [me]
    dests += [((mine[0] + way) & MASK) * RING + mine[1] for way in range(1, RING)]
    dests += [mine[0] * RING + ((mine[1] + way) & MASK) for way in range(1, RING)]

    @pl.loop(0, ngx)
    def _(i):
        for n in range(len(dests)):
            seen[n, i] = 0

    for half in range(2):
        for kind in range(2 * RING):
            count[half, kind] = 0
        for way in range(RING - 1):
            for rel in range(RING):
                for i in range(cap):
                    send[half, way, rel, i] = 0

    @pl.loop(0, nblk)
    def _(q):
        for l in range(nlinks):
            for n, dest in enumerate(dests):
                d = dev[dest, 0, q, l]
                at = (d >> BITS, d & MASK)
                i = seen[n, d]
                seen[n, d] = i + 1
                i = jnp.minimum(i, cap - 1)
                if n:
                    half, way = (n - 1) // (RING - 1), (n - 1) % (RING - 1)

                    @pl.when(at[half] == mine[half])
                    def _(half=half, way=way, at=at, i=i, dest=dest):
                        rel = (at[1 - half] - mine[1 - half]) & MASK
                        send[half, way, rel, i] = blk[dest, 0, q, l]

                    continue
                for half in range(2):
                    way = (at[half] - mine[half]) & MASK
                    rel = (at[1 - half] - mine[1 - half]) & MASK
                    own = blk[me, 0, q, l]
                    upper = (rel == RING // 2) & (own >= nblk // 2)
                    kind = jnp.where(way == 0, jnp.where(upper, 2 * RING - 1, rel), RING + way - 1)
                    place = jnp.where(way == 0, jnp.where(upper, own - nblk // 2, own), rel * cap + i)
                    k = count[half, kind]
                    far[half, kind, jnp.minimum(k, RING * cap - 1)] = place * 64 + q * nlinks + l
                    count[half, kind] = k + 1

    swap = band & 1
    void = nblk + 2 * cols
    nbeside[0] = 0

    @pl.loop(0, rows)
    def _(r0):
        for c0 in range(cols):
            for k in range(nstencil):
                r, t = r0 + offs[k, 0], c0 + offs[k, 1]
                code = jnp.where(r < 0, nblk + t, jnp.where(r >= rows, nblk + cols + t, r * cols + t))
                out = (r < 0) & (me == 0) | (r >= rows) & (me == ngx - 1)
                left, right = t < 0, t >= cols
                term = (r0 * cols + c0) * nstencil + k
                near[term] = jnp.where(out | left | right, void, code)
                if c0 in (0, cols - 1):
                    out = out | left & (band == 0) | right & (band == ngy - 1)

                    @pl.when((left | right) & jnp.logical_not(out))
                    def _(left=left, r=r, c0=c0, k=k):
                        n = nbeside[0]
                        which = jnp.where(left, 1 - swap, swap)
                        beside[n] = (((r0 * cols + c0) * 8 + k) * 64) + which * (rows + 2) + r + 1
                        nbeside[0] = n + 1


def pack_kernel(cap, send, *refs):
    nsrc, nout = 2 * (RING + 1), 2 * (RING - 1)
    srcs, outs = refs[:nsrc], refs[nsrc : nsrc + nout]
    pool, slots, sem, osem = refs[nsrc + nout :]
    loads, at = [], 0
    for i, src in enumerate(srcs):
        half = i // (RING + 1)
        at = 0 if i % (RING + 1) == 0 else at
        n = src.shape[0]
        loads.append(pltpu.make_async_copy(src, pool.at[half, pl.ds(at, n)], sem.at[i]))
        at += n
    for c in loads:
        c.start()
    nblk = srcs[0].shape[0]
    puts = []
    for half in range(2):
        for c in loads[half * (RING + 1) : (half + 1) * (RING + 1)]:
            c.wait()
        for way in range(RING - 1):
            n = half * (RING - 1) + way
            for rel in range(RING):
                for i in range(cap):
                    slots[n, rel * cap + i] = pool[half, rel * nblk + send[half, way, rel, i]]
            puts.append(pltpu.make_async_copy(slots.at[n], outs[n], osem.at[n]))
            puts[-1].start()
    for c in puts:
        c.wait()


def near_kernel(dims, nrim, grams, t, near, own_ref, *refs):
    nblk, nstencil, nsrc = dims
    rims, refs = refs[: len(nrim)], list(refs[len(nrim) :])
    w_ref, drive_ref = refs[:2]
    refs = refs[2:]
    gram_ref = refs.pop(0) if grams else None
    pre_ref = refs.pop(0)
    gram_out = refs.pop(0) if grams else None
    pool, wst, wdr, dr, pre, *refs = refs
    gin, gout = (refs.pop(0), refs.pop(0)) if grams else (None, None)
    sem, osem = refs
    units = own_ref.shape[-1]
    copies, at = [pltpu.make_async_copy(own_ref, pool.at[pl.ds(0, nblk)], sem.at[nblk])], nblk
    for i, n in enumerate(nrim):
        copies.append(pltpu.make_async_copy(rims[i], pool.at[pl.ds(at, n)], sem.at[nblk + i + 1]))
        at += n

    def ins(q):
        yield pltpu.make_async_copy(w_ref.at[q, pl.ds(0, nstencil)], wst.at[q], sem.at[q])
        yield pltpu.make_async_copy(w_ref.at[q, nsrc], wdr.at[q], sem.at[q])
        yield pltpu.make_async_copy(drive_ref.at[t, q], dr.at[q], sem.at[q])
        if grams:
            yield pltpu.make_async_copy(gram_ref.at[q], gin.at[q], sem.at[q])

    def puts(q):
        yield pltpu.make_async_copy(pre.at[q], pre_ref.at[q], osem.at[q])
        if grams:
            yield pltpu.make_async_copy(gout.at[q], gram_out.at[q], osem.at[q])

    for c in copies:
        c.start()

    @pl.loop(0, nblk)
    def _(q):
        for c in ins(q):
            c.start()

    pool[at] = jnp.zeros_like(pool[at])
    for c in copies:
        c.wait()

    @pl.loop(0, nblk)
    def _(q):
        for c in ins(q):
            c.wait()
        lhs = jnp.concatenate([pool[near[q * nstencil + k]] for k in range(nstencil)] + [dr[q]], axis=1)
        w = jnp.concatenate([wst[q].reshape(nstencil * units, units), wdr[q]], axis=0)
        pre[q] = jnp.dot(lhs, w, preferred_element_type=jnp.float32)
        if grams:
            x = pool[q]
            gout[q] = gin[q] + lax.dot_general(x, x, (((0,), (0,)), ((), ())), preferred_element_type=jnp.float32)
        for c in puts(q):
            c.start()

    @pl.loop(0, nblk)
    def _(q):
        for c in puts(q):
            c.wait()


def far_kernel(dims, last, far, count, beside, nbeside, *refs):
    nblk, h, nstencil, nlinks = dims
    nin = 4 * RING
    bufs, refs = refs[:nin], list(refs[nin:])
    core_ref, side_ref, own_ref, w_ref, pre_ref, leak_ref = refs[:6]
    refs = refs[6:]
    gram_ref = refs.pop(0) if last else None
    nout = 2 if last else 3
    outs, refs = refs[:nout], refs[nout:]
    got, cols, wb, old, wl, pre, new, *refs = refs
    gin, gout = (refs.pop(0), refs.pop(0)) if last else (None, None)
    sem, osem, bsem = refs
    tall = core_ref.shape[0]
    whole = [
        pltpu.make_async_copy(pre_ref, pre, sem.at[nblk + 1]),
        pltpu.make_async_copy(core_ref, cols.at[pl.ds(0, tall)], sem.at[nblk + 2]),
        pltpu.make_async_copy(side_ref, cols.at[pl.ds(tall, tall)], sem.at[nblk + 3]),
    ]
    for c in whole:
        c.start()

    def weight(n):
        e = beside[n]
        return pltpu.make_async_copy(w_ref.at[e >> 9, (e >> 6) & 7], wb.at[n], bsem.at[n])

    @pl.loop(0, nbeside[0])
    def _(n):
        weight(n).start()

    for half in range(2):
        for kind in range(2 * RING):
            src = bufs[half * 2 * RING + kind]

            @pl.loop(0, count[half, kind])
            def _(n, half=half, kind=kind, src=src):
                e = far[half, kind, n]
                to = got.at[e & 63, pl.ds(half * h, h)]
                pltpu.make_async_copy(src.at[e >> 6], to, sem.at[nblk]).start()

    def ins(q):
        yield pltpu.make_async_copy(own_ref.at[q], old.at[q], sem.at[q])
        yield pltpu.make_async_copy(w_ref.at[q, pl.ds(nstencil, nlinks)], wl.at[q], sem.at[q])
        if last:
            yield pltpu.make_async_copy(gram_ref.at[q], gin.at[q], sem.at[q])

    def puts(q):
        if last:
            yield pltpu.make_async_copy(new.at[q], outs[0].at[q], osem.at[q])
            yield pltpu.make_async_copy(gout.at[q], outs[1].at[q], osem.at[q])
        else:
            yield pltpu.make_async_copy(new.at[q, pl.ds(0, h)], outs[0].at[q], osem.at[q])
            yield pltpu.make_async_copy(new.at[q, pl.ds(h, h)], outs[1].at[q], osem.at[q])
            yield pltpu.make_async_copy(new.at[q], outs[2].at[q], osem.at[q])

    @pl.loop(0, nblk)
    def _(q):
        for c in ins(q):
            c.start()

    for c in whole:
        c.wait()

    @pl.loop(0, nbeside[0])
    def _(n):
        weight(n).wait()
        e = beside[n]
        pre[e >> 9] += jnp.dot(cols[e & 63], wb[n], preferred_element_type=jnp.float32)

    pltpu.make_async_copy(got, got, sem.at[nblk]).wait()

    group = 3
    units = wl.shape[-1]

    @pl.loop(0, nblk // group)
    def _(i):
        qs = [i * group + j for j in range(group)]
        for q in qs:
            for c in ins(q):
                c.wait()
        fresh = []
        for q in qs:
            lhs = jnp.concatenate([got[q * nlinks + l] for l in range(nlinks)], axis=1)
            w = wl[q].reshape(nlinks * units, units)
            total = pre[q] + jnp.dot(lhs, w, preferred_element_type=jnp.float32)
            rate = leak_ref[pl.ds(q, 1), :]
            fresh.append(((1.0 - rate) * old[q].astype(jnp.float32) + rate * jnp.tanh(total)).astype(jnp.bfloat16))
        for q, x in zip(qs, fresh):
            new[q] = x
            if last:
                gout[q] = gin[q] + lax.dot_general(x, x, (((0,), (0,)), ((), ())), preferred_element_type=jnp.float32)
        for q in qs:
            for c in puts(q):
                c.start()

    @pl.loop(0, nblk)
    def _(q):
        for c in puts(q):
            c.wait()


def after(x, *done):
    return lax.optimization_barrier((x, *done))[0]


def shards(state, weights, drive, leak, link_dev, link_blk, offsets, gram_prev):
    rows, cols, seq, units = state.shape
    nblk = rows * cols
    nlinks = link_dev.shape[-1]
    nstencil = offsets.shape[0]
    ngx = RING * RING
    cap = 4
    slots = RING * cap
    steps = drive.shape[0]
    gx = ("x", "y")
    gy = ("z", "core")
    ny = lax.axis_size(gy)
    nsrc = nstencil + nlinks
    bf16 = jnp.bfloat16
    f32 = jnp.float32
    h = seq // 2
    params = pltpu.CompilerParams(vmem_limit_bytes=VMEM_BYTES)
    kinds = 2 * RING
    pos = jnp.stack([lax.axis_index(gx), lax.axis_index(gy)]).astype(jnp.int32)
    send, near, far, count, beside, nbeside = pl.pallas_call(
        functools.partial(plan_kernel, (rows, cols, nlinks, nstencil, cap, ngx, ny)),
        out_shape=(
            jax.ShapeDtypeStruct((2, RING - 1, RING, cap), jnp.int32),
            jax.ShapeDtypeStruct((nblk * nstencil,), jnp.int32),
            jax.ShapeDtypeStruct((2, kinds, slots), jnp.int32),
            jax.ShapeDtypeStruct((2, kinds), jnp.int32),
            jax.ShapeDtypeStruct((rows * nstencil,), jnp.int32),
            jax.ShapeDtypeStruct((1,), jnp.int32),
        ),
        in_specs=[SMEM] * 4,
        out_specs=(SMEM,) * 6,
        scratch_shapes=[pltpu.SMEM((2 * RING - 1, ngx), jnp.int32)],
        name="plan",
    )(pos, link_dev, link_blk, offsets)

    state = state.reshape(nblk, seq, units)
    weights = weights.reshape(nblk, nsrc + 1, units, units)
    drive = drive.reshape(steps, nblk, seq, units)
    leak = leak.reshape(nblk, units)
    gram = gram_prev.reshape(nblk, units, units)

    def shift(x, axis, k):
        return lax.ppermute(x, axis, [(i, (i - k) % RING) for i in range(RING)])

    def ring(x, k):
        return lax.ppermute(x, gx, [(i, (i + k) % ngx) for i in range(ngx)])

    def first(a, b, full):
        grid = full.reshape(rows, cols, seq, units)
        y1, y3 = shift(a, "y", 1), shift(a, "y", 3)
        x1, x3 = shift(b, "x", 1), shift(b, "x", 3)
        m = nblk // 2
        done = (y1, y3, x1, x3, count)
        y2l, y2u = shift(after(y1[:m], *done), "y", 1), shift(after(y3[m:], *done), "y", 3)
        x2l, x2u = shift(after(x1[:m], *done), "x", 1), shift(after(x3[m:], *done), "x", 3)
        above, below = ring(after(grid[rows - 1], *done), 1), ring(after(grid[0], *done), -1)
        a = [after(a, above, below), y1, y2l, y2u, y3]
        return a, [b, x1, x2l, x2u, x3], above, below

    def pack(a, b):
        return pl.pallas_call(
            functools.partial(pack_kernel, cap),
            out_shape=[jax.ShapeDtypeStruct((slots, h, units), bf16)] * (2 * (RING - 1)),
            in_specs=[SMEM] + [ANY] * (len(a) + len(b)),
            out_specs=[ANY] * (2 * (RING - 1)),
            scratch_shapes=[
                pltpu.VMEM((2, RING * nblk, h, units), bf16),
                pltpu.VMEM((2 * (RING - 1), slots, h, units), bf16),
                pltpu.SemaphoreType.DMA((len(a) + len(b),)),
                pltpu.SemaphoreType.DMA((2 * (RING - 1),)),
            ],
            compiler_params=params,
            name="pack",
        )(send, *a, *b)

    def second(packed, full, above, below, work):
        pa, pb = packed[: RING - 1], packed[RING - 1 :]
        x1, x3 = shift(pa[2], "x", 1), shift(pa[0], "x", 3)
        y1, y3 = shift(pb[2], "y", 1), shift(pb[0], "y", 3)
        res = work()
        x2, y2 = shift(after(pa[1], x1, x3, res[0]), "x", 2), shift(after(pb[1], y1, y3, res[0]), "y", 2)
        grid = full.reshape(rows, cols, seq, units)
        tall = lambda c: jnp.concatenate([above[c : c + 1], grid[:, c], below[c : c + 1]], axis=0)
        even = lax.axis_index("core") == 0
        chip, step = jnp.where(even, tall(cols - 1), tall(0)), jnp.where(even, tall(0), tall(cols - 1))
        core = lax.ppermute(after(chip, res[0]), gy, [(i, i + 1 - 2 * (i % 2)) for i in range(ny)])
        side = lax.ppermute(after(step, res[0]), gy, [(i, (i - 1 + 2 * (i % 2)) % ny) for i in range(ny)])
        return [x1, x2, x3], [y1, y2, y3], core, side, res

    def products(t, full, rim, gram):
        nrim = tuple(r.shape[0] for r in rim)
        args = [near, full, *rim, weights, drive]
        outs = [jax.ShapeDtypeStruct((nblk, seq, units), f32)]
        scratch = [
            pltpu.VMEM((nblk + sum(nrim) + 1, seq, units), bf16),
            pltpu.VMEM((nblk, nstencil, units, units), bf16),
            pltpu.VMEM((nblk, units, units), bf16),
            pltpu.VMEM((nblk, seq, units), bf16),
            pltpu.VMEM((nblk, seq, units), f32),
        ]
        if gram is not None:
            args.append(gram)
            outs.append(jax.ShapeDtypeStruct((nblk, units, units), f32))
            scratch += [pltpu.VMEM((nblk, units, units), f32)] * 2
        scratch += [pltpu.SemaphoreType.DMA((nblk + 1 + len(nrim),)), pltpu.SemaphoreType.DMA((nblk,))]
        return pl.pallas_call(
            functools.partial(near_kernel, (nblk, nstencil, nsrc), nrim, gram is not None, t),
            out_shape=outs,
            in_specs=[SMEM] + [ANY] * (len(args) - 1),
            out_specs=[ANY] * len(outs),
            scratch_shapes=scratch,
            compiler_params=params,
            name="near",
        )(*args)

    def finish(a, b, ga, gb, core, side, full, pre, gram, last):
        args = [far, count, beside, nbeside]
        for x, g in ((a, ga), (b, gb)):
            args += [*x[:3], x[4], *g, x[3]]
        args += [core, side, full, weights, pre, leak]
        in_specs = [SMEM] * 4 + [ANY] * (len(args) - 5) + [VMEM]
        scratch = [
            pltpu.VMEM((nblk * nlinks, seq, units), bf16),
            pltpu.VMEM((2 * (rows + 2), seq, units), bf16),
            pltpu.VMEM((rows * nstencil, units, units), bf16),
            pltpu.VMEM((nblk, seq, units), bf16),
            pltpu.VMEM((nblk, nlinks, units, units), bf16),
            pltpu.VMEM((nblk, seq, units), f32),
            pltpu.VMEM((nblk, seq, units), bf16),
        ]
        if last:
            args.append(gram)
            in_specs.append(ANY)
            outs = [jax.ShapeDtypeStruct((nblk, seq, units), bf16), jax.ShapeDtypeStruct((nblk, units, units), f32)]
            scratch += [pltpu.VMEM((nblk, units, units), f32)] * 2
        else:
            outs = [jax.ShapeDtypeStruct((nblk, n, units), bf16) for n in (h, h, seq)]
        scratch += [pltpu.SemaphoreType.DMA((n,)) for n in (nblk + 4, nblk, rows * nstencil)]
        return pl.pallas_call(
            functools.partial(far_kernel, (nblk, h, nstencil, nlinks), last),
            out_shape=outs,
            in_specs=in_specs,
            out_specs=[ANY] * len(outs),
            scratch_shapes=scratch,
            compiler_params=params,
            name="far",
        )(*args)

    own_a, own_b, full = state[:, :h], state[:, h:], state
    for t in range(steps):
        a, b, above, below = first(own_a, own_b, full)
        packed = pack(a, b)
        work = lambda: products(t, after(full, packed[0]), [above, below], gram if t else None)
        ga, gb, core, side, res = second(packed, full, above, below, work)
        pre = res[0]
        if t:
            gram = res[1]
        res = finish(a, b, ga, gb, core, side, full, pre, gram, t == steps - 1)
        if t < steps - 1:
            own_a, own_b, full = res
    final, gram = res
    return final.reshape(rows, cols, seq, units), gram.reshape(rows, cols, units, units)


def solution(mesh):
    grid = Mesh(mesh.devices.reshape(4, 4, 4, 2), ("x", "y", "z", "core"))
    gx, gy = ("x", "y"), ("z", "core")
    return jax.shard_map(
        shards,
        mesh=grid,
        in_specs=(
            P(gx, gy, None, None),
            P(gx, gy, None, None, None),
            P(None, gx, gy, None, None),
            P(gx, gy, None),
            P(None, gy, None, None),
            P(None, gy, None, None),
            P(),
            P(gx, gy, None, None),
        ),
        out_specs=(P(gx, gy, None, None), P(gx, gy, None, None)),
        check_vma=False,
    )
```

```python
import functools

import jax
import jax.numpy as jnp
from jax import lax
from jax.experimental import pallas as pl
from jax.experimental.pallas import tpu as pltpu
from jax.sharding import Mesh, PartitionSpec as P

VMEM_BYTES = 56 * 1024 * 1024
ANY = pl.BlockSpec(memory_space=pl.ANY)
SMEM = pl.BlockSpec(memory_space=pltpu.SMEM)
VMEM = pl.BlockSpec(memory_space=pltpu.VMEM)
RING = 4
BITS, MASK = 2, RING - 1


def plan_kernel(dims, pos, dev, blk, offs, send, near, far, count, beside, nbeside, seen):
    rows, cols, nlinks, nstencil, cap, ngx, ngy = dims
    nblk = rows * cols
    me, band = pos[0], pos[1]
    mine = (me >> BITS, me & MASK)
    dests = [me]
    dests += [((mine[0] + way) & MASK) * RING + mine[1] for way in range(1, RING)]
    dests += [mine[0] * RING + ((mine[1] + way) & MASK) for way in range(1, RING)]

    @pl.loop(0, ngx)
    def _(i):
        for n in range(len(dests)):
            seen[n, i] = 0

    for half in range(2):
        for kind in range(2 * RING):
            count[half, kind] = 0
        for way in range(RING - 1):
            for rel in range(RING):
                for i in range(cap):
                    send[half, way, rel, i] = 0

    @pl.loop(0, nblk)
    def _(q):
        for l in range(nlinks):
            for n, dest in enumerate(dests):
                d = dev[dest, 0, q, l]
                at = (d >> BITS, d & MASK)
                i = seen[n, d]
                seen[n, d] = i + 1
                i = jnp.minimum(i, cap - 1)
                if n:
                    half, way = (n - 1) // (RING - 1), (n - 1) % (RING - 1)

                    @pl.when(at[half] == mine[half])
                    def _(half=half, way=way, at=at, i=i, dest=dest):
                        rel = (at[1 - half] - mine[1 - half]) & MASK
                        send[half, way, rel, i] = blk[dest, 0, q, l]

                    continue
                for half in range(2):
                    way = (at[half] - mine[half]) & MASK
                    rel = (at[1 - half] - mine[1 - half]) & MASK
                    own = blk[me, 0, q, l]
                    upper = (rel == RING // 2) & (own >= nblk // 2)
                    kind = jnp.where(way == 0, jnp.where(upper, 2 * RING - 1, rel), RING + way - 1)
                    place = jnp.where(way == 0, jnp.where(upper, own - nblk // 2, own), rel * cap + i)
                    k = count[half, kind]
                    far[half, kind, jnp.minimum(k, RING * cap - 1)] = place * 64 + q * nlinks + l
                    count[half, kind] = k + 1

    swap = band & 1
    void = nblk + 2 * cols
    nbeside[0] = 0

    @pl.loop(0, rows)
    def _(r0):
        for c0 in range(cols):
            for k in range(nstencil):
                r, t = r0 + offs[k, 0], c0 + offs[k, 1]
                code = jnp.where(r < 0, nblk + t, jnp.where(r >= rows, nblk + cols + t, r * cols + t))
                out = (r < 0) & (me == 0) | (r >= rows) & (me == ngx - 1)
                left, right = t < 0, t >= cols
                term = (r0 * cols + c0) * nstencil + k
                near[term] = jnp.where(out | left | right, void, code)
                if c0 in (0, cols - 1):
                    out = out | left & (band == 0) | right & (band == ngy - 1)

                    @pl.when((left | right) & jnp.logical_not(out))
                    def _(left=left, r=r, c0=c0, k=k):
                        n = nbeside[0]
                        which = jnp.where(left, 1 - swap, swap)
                        beside[n] = (((r0 * cols + c0) * 8 + k) * 64) + which * (rows + 2) + r + 1
                        nbeside[0] = n + 1


def pack_kernel(cap, send, *refs):
    nsrc, nout = 2 * (RING + 1), 2 * (RING - 1)
    srcs, outs = refs[:nsrc], refs[nsrc : nsrc + nout]
    pool, slots, sem, osem = refs[nsrc + nout :]
    loads, at = [], 0
    for i, src in enumerate(srcs):
        half = i // (RING + 1)
        at = 0 if i % (RING + 1) == 0 else at
        n = src.shape[0]
        loads.append(pltpu.make_async_copy(src, pool.at[half, pl.ds(at, n)], sem.at[i]))
        at += n
    for c in loads:
        c.start()
    nblk = srcs[0].shape[0]
    puts = []
    for half in range(2):
        for c in loads[half * (RING + 1) : (half + 1) * (RING + 1)]:
            c.wait()
        for way in range(RING - 1):
            n = half * (RING - 1) + way
            for rel in range(RING):
                for i in range(cap):
                    slots[n, rel * cap + i] = pool[half, rel * nblk + send[half, way, rel, i]]
            puts.append(pltpu.make_async_copy(slots.at[n], outs[n], osem.at[n]))
            puts[-1].start()
    for c in puts:
        c.wait()


def near_kernel(dims, nrim, grams, t, near, own_ref, *refs):
    nblk, nstencil, nsrc = dims
    rims, refs = refs[: len(nrim)], list(refs[len(nrim) :])
    w_ref, drive_ref = refs[:2]
    refs = refs[2:]
    gram_ref = refs.pop(0) if grams else None
    pre_ref = refs.pop(0)
    gram_out = refs.pop(0) if grams else None
    pool, wst, wdr, dr, pre, *refs = refs
    gin, gout = (refs.pop(0), refs.pop(0)) if grams else (None, None)
    sem, osem = refs
    units = own_ref.shape[-1]
    copies, at = [pltpu.make_async_copy(own_ref, pool.at[pl.ds(0, nblk)], sem.at[nblk])], nblk
    for i, n in enumerate(nrim):
        copies.append(pltpu.make_async_copy(rims[i], pool.at[pl.ds(at, n)], sem.at[nblk + i + 1]))
        at += n

    def ins(q):
        yield pltpu.make_async_copy(w_ref.at[q, pl.ds(0, nstencil)], wst.at[q], sem.at[q])
        yield pltpu.make_async_copy(w_ref.at[q, nsrc], wdr.at[q], sem.at[q])
        yield pltpu.make_async_copy(drive_ref.at[t, q], dr.at[q], sem.at[q])
        if grams:
            yield pltpu.make_async_copy(gram_ref.at[q], gin.at[q], sem.at[q])

    def puts(q):
        yield pltpu.make_async_copy(pre.at[q], pre_ref.at[q], osem.at[q])
        if grams:
            yield pltpu.make_async_copy(gout.at[q], gram_out.at[q], osem.at[q])

    for c in copies:
        c.start()

    @pl.loop(0, nblk)
    def _(q):
        for c in ins(q):
            c.start()

    pool[at] = jnp.zeros_like(pool[at])
    for c in copies:
        c.wait()

    @pl.loop(0, nblk)
    def _(q):
        for c in ins(q):
            c.wait()
        lhs = jnp.concatenate([pool[near[q * nstencil + k]] for k in range(nstencil)] + [dr[q]], axis=1)
        w = jnp.concatenate([wst[q].reshape(nstencil * units, units), wdr[q]], axis=0)
        pre[q] = jnp.dot(lhs, w, preferred_element_type=jnp.float32)
        if grams:
            x = pool[q]
            gout[q] = gin[q] + lax.dot_general(x, x, (((0,), (0,)), ((), ())), preferred_element_type=jnp.float32)
        for c in puts(q):
            c.start()

    @pl.loop(0, nblk)
    def _(q):
        for c in puts(q):
            c.wait()


def far_kernel(dims, last, far, count, beside, nbeside, *refs):
    nblk, h, nstencil, nlinks = dims
    nin = 4 * RING
    bufs, refs = refs[:nin], list(refs[nin:])
    core_ref, side_ref, own_ref, w_ref, pre_ref, leak_ref = refs[:6]
    refs = refs[6:]
    gram_ref = refs.pop(0) if last else None
    nout = 2 if last else 3
    outs, refs = refs[:nout], refs[nout:]
    got, cols, wb, old, wl, pre, new, *refs = refs
    gin, gout = (refs.pop(0), refs.pop(0)) if last else (None, None)
    sem, osem, bsem = refs
    tall = core_ref.shape[0]
    whole = [
        pltpu.make_async_copy(pre_ref, pre, sem.at[nblk + 1]),
        pltpu.make_async_copy(core_ref, cols.at[pl.ds(0, tall)], sem.at[nblk + 2]),
        pltpu.make_async_copy(side_ref, cols.at[pl.ds(tall, tall)], sem.at[nblk + 3]),
    ]
    for half in range(2):
        for kind in range(2 * RING):
            src = bufs[half * 2 * RING + kind]

            @pl.loop(0, count[half, kind])
            def _(n, half=half, kind=kind, src=src):
                e = far[half, kind, n]
                to = got.at[e & 63, pl.ds(half * h, h)]
                pltpu.make_async_copy(src.at[e >> 6], to, sem.at[nblk]).start()

    for c in whole:
        c.start()

    def weight(n):
        e = beside[n]
        return pltpu.make_async_copy(w_ref.at[e >> 9, (e >> 6) & 7], wb.at[n], bsem.at[n])

    @pl.loop(0, nbeside[0])
    def _(n):
        weight(n).start()

    def ins(q):
        yield pltpu.make_async_copy(own_ref.at[q], old.at[q], sem.at[q])
        yield pltpu.make_async_copy(w_ref.at[q, pl.ds(nstencil, nlinks)], wl.at[q], sem.at[q])
        if last:
            yield pltpu.make_async_copy(gram_ref.at[q], gin.at[q], sem.at[q])

    def puts(q):
        if last:
            yield pltpu.make_async_copy(new.at[q], outs[0].at[q], osem.at[q])
            yield pltpu.make_async_copy(gout.at[q], outs[1].at[q], osem.at[q])
        else:
            yield pltpu.make_async_copy(new.at[q, pl.ds(0, h)], outs[0].at[q], osem.at[q])
            yield pltpu.make_async_copy(new.at[q, pl.ds(h, h)], outs[1].at[q], osem.at[q])
            yield pltpu.make_async_copy(new.at[q], outs[2].at[q], osem.at[q])

    @pl.loop(0, nblk)
    def _(q):
        for c in ins(q):
            c.start()

    for c in whole:
        c.wait()

    @pl.loop(0, nbeside[0])
    def _(n):
        weight(n).wait()
        e = beside[n]
        pre[e >> 9] += jnp.dot(cols[e & 63], wb[n], preferred_element_type=jnp.float32)

    pltpu.make_async_copy(got, got, sem.at[nblk]).wait()

    group = 4
    units = wl.shape[-1]

    @pl.loop(0, nblk // group)
    def _(i):
        qs = [i * group + j for j in range(group)]
        for q in qs:
            for c in ins(q):
                c.wait()
        fresh = []
        for q in qs:
            lhs = jnp.concatenate([got[q * nlinks + l] for l in range(nlinks)], axis=1)
            w = wl[q].reshape(nlinks * units, units)
            total = pre[q] + jnp.dot(lhs, w, preferred_element_type=jnp.float32)
            rate = leak_ref[pl.ds(q, 1), :]
            fresh.append(((1.0 - rate) * old[q].astype(jnp.float32) + rate * jnp.tanh(total)).astype(jnp.bfloat16))
        for q, x in zip(qs, fresh):
            new[q] = x
            if last:
                gout[q] = gin[q] + lax.dot_general(x, x, (((0,), (0,)), ((), ())), preferred_element_type=jnp.float32)
        for q in qs:
            for c in puts(q):
                c.start()

    @pl.loop(0, nblk)
    def _(q):
        for c in puts(q):
            c.wait()


def after(x, *done):
    return lax.optimization_barrier((x, *done))[0]


def shards(state, weights, drive, leak, link_dev, link_blk, offsets, gram_prev):
    rows, cols, seq, units = state.shape
    nblk = rows * cols
    nlinks = link_dev.shape[-1]
    nstencil = offsets.shape[0]
    ngx = RING * RING
    cap = 4
    slots = RING * cap
    steps = drive.shape[0]
    gx = ("x", "y")
    gy = ("z", "core")
    ny = lax.axis_size(gy)
    nsrc = nstencil + nlinks
    bf16 = jnp.bfloat16
    f32 = jnp.float32
    h = seq // 2
    params = pltpu.CompilerParams(vmem_limit_bytes=VMEM_BYTES)
    kinds = 2 * RING
    pos = jnp.stack([lax.axis_index(gx), lax.axis_index(gy)]).astype(jnp.int32)
    send, near, far, count, beside, nbeside = pl.pallas_call(
        functools.partial(plan_kernel, (rows, cols, nlinks, nstencil, cap, ngx, ny)),
        out_shape=(
            jax.ShapeDtypeStruct((2, RING - 1, RING, cap), jnp.int32),
            jax.ShapeDtypeStruct((nblk * nstencil,), jnp.int32),
            jax.ShapeDtypeStruct((2, kinds, slots), jnp.int32),
            jax.ShapeDtypeStruct((2, kinds), jnp.int32),
            jax.ShapeDtypeStruct((rows * nstencil,), jnp.int32),
            jax.ShapeDtypeStruct((1,), jnp.int32),
        ),
        in_specs=[SMEM] * 4,
        out_specs=(SMEM,) * 6,
        scratch_shapes=[pltpu.SMEM((2 * RING - 1, ngx), jnp.int32)],
        name="plan",
    )(pos, link_dev, link_blk, offsets)

    state = state.reshape(nblk, seq, units)
    weights = weights.reshape(nblk, nsrc + 1, units, units)
    drive = drive.reshape(steps, nblk, seq, units)
    leak = leak.reshape(nblk, units)
    gram = gram_prev.reshape(nblk, units, units)

    def shift(x, axis, k):
        return lax.ppermute(x, axis, [(i, (i - k) % RING) for i in range(RING)])

    def ring(x, k):
        return lax.ppermute(x, gx, [(i, (i + k) % ngx) for i in range(ngx)])

    def first(a, b, full):
        grid = full.reshape(rows, cols, seq, units)
        y1, y3 = shift(a, "y", 1), shift(a, "y", 3)
        x1, x3 = shift(b, "x", 1), shift(b, "x", 3)
        m = nblk // 2
        done = (y1, y3, x1, x3, count)
        y2l, y2u = shift(after(y1[:m], *done), "y", 1), shift(after(y3[m:], *done), "y", 3)
        x2l, x2u = shift(after(x1[:m], *done), "x", 1), shift(after(x3[m:], *done), "x", 3)
        above, below = ring(after(grid[rows - 1], *done), 1), ring(after(grid[0], *done), -1)
        a = [after(a, above, below), y1, y2l, y2u, y3]
        return a, [b, x1, x2l, x2u, x3], above, below

    def pack(a, b):
        return pl.pallas_call(
            functools.partial(pack_kernel, cap),
            out_shape=[jax.ShapeDtypeStruct((slots, h, units), bf16)] * (2 * (RING - 1)),
            in_specs=[SMEM] + [ANY] * (len(a) + len(b)),
            out_specs=[ANY] * (2 * (RING - 1)),
            scratch_shapes=[
                pltpu.VMEM((2, RING * nblk, h, units), bf16),
                pltpu.VMEM((2 * (RING - 1), slots, h, units), bf16),
                pltpu.SemaphoreType.DMA((len(a) + len(b),)),
                pltpu.SemaphoreType.DMA((2 * (RING - 1),)),
            ],
            compiler_params=params,
            name="pack",
        )(send, *a, *b)

    def second(packed, full, above, below, work):
        pa, pb = packed[: RING - 1], packed[RING - 1 :]
        x1, x3 = shift(pa[2], "x", 1), shift(pa[0], "x", 3)
        y1, y3 = shift(pb[2], "y", 1), shift(pb[0], "y", 3)
        res = work()
        x2, y2 = shift(after(pa[1], x1, x3, res[0]), "x", 2), shift(after(pb[1], y1, y3, res[0]), "y", 2)
        grid = full.reshape(rows, cols, seq, units)
        tall = lambda c: jnp.concatenate([above[c : c + 1], grid[:, c], below[c : c + 1]], axis=0)
        even = lax.axis_index("core") == 0
        chip, step = jnp.where(even, tall(cols - 1), tall(0)), jnp.where(even, tall(0), tall(cols - 1))
        core = lax.ppermute(after(chip, res[0]), gy, [(i, i + 1 - 2 * (i % 2)) for i in range(ny)])
        side = lax.ppermute(after(step, res[0]), gy, [(i, (i - 1 + 2 * (i % 2)) % ny) for i in range(ny)])
        return [x1, x2, x3], [y1, y2, y3], core, side, res

    def products(t, full, rim, gram):
        nrim = tuple(r.shape[0] for r in rim)
        args = [near, full, *rim, weights, drive]
        outs = [jax.ShapeDtypeStruct((nblk, seq, units), f32)]
        scratch = [
            pltpu.VMEM((nblk + sum(nrim) + 1, seq, units), bf16),
            pltpu.VMEM((nblk, nstencil, units, units), bf16),
            pltpu.VMEM((nblk, units, units), bf16),
            pltpu.VMEM((nblk, seq, units), bf16),
            pltpu.VMEM((nblk, seq, units), f32),
        ]
        if gram is not None:
            args.append(gram)
            outs.append(jax.ShapeDtypeStruct((nblk, units, units), f32))
            scratch += [pltpu.VMEM((nblk, units, units), f32)] * 2
        scratch += [pltpu.SemaphoreType.DMA((nblk + 1 + len(nrim),)), pltpu.SemaphoreType.DMA((nblk,))]
        return pl.pallas_call(
            functools.partial(near_kernel, (nblk, nstencil, nsrc), nrim, gram is not None, t),
            out_shape=outs,
            in_specs=[SMEM] + [ANY] * (len(args) - 1),
            out_specs=[ANY] * len(outs),
            scratch_shapes=scratch,
            compiler_params=params,
            name="near",
        )(*args)

    def finish(a, b, ga, gb, core, side, full, pre, gram, last):
        args = [far, count, beside, nbeside]
        for x, g in ((a, ga), (b, gb)):
            args += [*x[:3], x[4], *g, x[3]]
        args += [core, side, full, weights, pre, leak]
        in_specs = [SMEM] * 4 + [ANY] * (len(args) - 5) + [VMEM]
        scratch = [
            pltpu.VMEM((nblk * nlinks, seq, units), bf16),
            pltpu.VMEM((2 * (rows + 2), seq, units), bf16),
            pltpu.VMEM((rows * nstencil, units, units), bf16),
            pltpu.VMEM((nblk, seq, units), bf16),
            pltpu.VMEM((nblk, nlinks, units, units), bf16),
            pltpu.VMEM((nblk, seq, units), f32),
            pltpu.VMEM((nblk, seq, units), bf16),
        ]
        if last:
            args.append(gram)
            in_specs.append(ANY)
            outs = [jax.ShapeDtypeStruct((nblk, seq, units), bf16), jax.ShapeDtypeStruct((nblk, units, units), f32)]
            scratch += [pltpu.VMEM((nblk, units, units), f32)] * 2
        else:
            outs = [jax.ShapeDtypeStruct((nblk, n, units), bf16) for n in (h, h, seq)]
        scratch += [pltpu.SemaphoreType.DMA((n,)) for n in (nblk + 4, nblk, rows * nstencil)]
        return pl.pallas_call(
            functools.partial(far_kernel, (nblk, h, nstencil, nlinks), last),
            out_shape=outs,
            in_specs=in_specs,
            out_specs=[ANY] * len(outs),
            scratch_shapes=scratch,
            compiler_params=params,
            name="far",
        )(*args)

    own_a, own_b, full = state[:, :h], state[:, h:], state
    for t in range(steps):
        a, b, above, below = first(own_a, own_b, full)
        packed = pack(a, b)
        work = lambda: products(t, after(full, packed[0]), [above, below], gram if t else None)
        ga, gb, core, side, res = second(packed, full, above, below, work)
        pre = res[0]
        if t:
            gram = res[1]
        res = finish(a, b, ga, gb, core, side, full, pre, gram, t == steps - 1)
        if t < steps - 1:
            own_a, own_b, full = res
    final, gram = res
    return final.reshape(rows, cols, seq, units), gram.reshape(rows, cols, units, units)


def solution(mesh):
    grid = Mesh(mesh.devices.reshape(4, 4, 4, 2), ("x", "y", "z", "core"))
    gx, gy = ("x", "y"), ("z", "core")
    return jax.shard_map(
        shards,
        mesh=grid,
        in_specs=(
            P(gx, gy, None, None),
            P(gx, gy, None, None, None),
            P(None, gx, gy, None, None),
            P(gx, gy, None),
            P(None, gy, None, None),
            P(None, gy, None, None),
            P(),
            P(gx, gy, None, None),
        ),
        out_specs=(P(gx, gy, None, None), P(gx, gy, None, None)),
        check_vma=False,
    )
```
